512 devices in a mesh: sector: 32 (over z, core), chan: 16 (over x, y).
Axes of the slice: x: 4, y: 4, z: 16, core: 2. Of those that a mesh axis runs over, the one named last changes fastest.
Arguments:
- wavefunc: float32 [128, 256, 256], P('sector', 'chan'), may hold values from -6 to 6
- left_env: float32 [32, 128, 256, 256], P('chan', 'sector'), may hold values from -0.375 to 0.375
- right_env: float32 [32, 128, 256, 256], P('chan', 'sector'), may hold values from -0.375 to 0.375
- source: int32 [5, 128], replicated, may hold values from 0 to 127, as said below
- shift_class: int32 [32], replicated, may hold values from 0 to 4
- channel_block_mask: int32 [32, 128], replicated, may hold values 0 or 1
- block_size: int32 [128], replicated, may hold values from 128 to 256
Outputs:
- sigma: float32 [128, 256, 256], P('sector', 'chan')
The draws below stay inside these ranges and needn't reach their ends.
Inputs may be any that keep to these rules, and one draw needn't show every extreme that they name: source[q, t] differs from t by at most 4.
All inputs are finite; a program needn't handle non-finite values.
Results may differ from the reference program's by a relative error of at most 0.0001.
Values sent between devices are 32-bit elements; how exact they have to be, the bound alone decides.
A program may use at most 64 MiB of HBM per device.

```python
import jax
import jax.numpy as jnp
from jax import lax

B = 256
SEC_DEV = 4
NSHIFT = 5
SECTORS = 128
CHANNELS = 32


def draw_source(key, part):
    key = jax.random.fold_in(key, 11)
    offsets = jax.random.randint(key, (NSHIFT, SECTORS), -SEC_DEV, SEC_DEV + 1)
    targets = jnp.arange(SECTORS, dtype=jnp.int32)
    return jnp.clip(targets[None, :] + offsets, 0, SECTORS - 1).astype(jnp.int32)


def place_ends(entries, rng, smallest, top_value):
    extent = entries.shape
    place = [jax.random.randint(jax.random.fold_in(rng, axis), (), 0, extent[axis]) for axis in range(len(extent))]
    entries = entries.at[tuple(place)].set(smallest)
    longest = extent.index(max(extent))
    place[longest] = (place[longest] + 1) % extent[longest]
    return entries.at[tuple(place)].set(top_value)


def shard_levels(key, dims, shards, low, high):
    gain, own = 1.0, jax.random.fold_in(key, 6)
    for dim, shards_of in shards:
        heights = jnp.exp(jax.random.uniform(jax.random.fold_in(own, dim), (shards_of,), jnp.float32, low / len(shards), high / len(shards)))
        gain = gain * jnp.repeat(heights, dims[dim] // shards_of).reshape([-1 if axis == dim else 1 for axis in range(len(dims))])
    return gain


def scatter_about(own_key, shape, deviation, limit, cuts=(), kind=jnp.bfloat16):
    array = deviation * jax.random.normal(own_key, shape, jnp.float32)
    if cuts:
        array = array * shard_levels(own_key, shape, cuts, -0.22, 0.18)
    return jnp.clip(array, -limit, limit).astype(kind)


def setup_inputs(seed: int = 0) -> dict:
    streams_of = jax.random.split(jax.random.key(seed), 8)
    wavefunc = scatter_about(streams_of[0], (SECTORS, B, B), 1.0, 6.0, ((0, 32), (1, 16)), jnp.float32)
    left_env = scatter_about(streams_of[1], (CHANNELS, SECTORS, B, B), B ** -0.5, 0.375, ((0, 16), (1, 32)), jnp.float32)
    right_env = scatter_about(streams_of[2], (CHANNELS, SECTORS, B, B), B ** -0.5, 0.375, ((0, 16), (1, 32)), jnp.float32)
    source = draw_source(jax.random.fold_in(streams_of[7], 71), 0)
    shift_class = place_ends(jax.random.randint(streams_of[4], (CHANNELS,), 0, NSHIFT), jax.random.fold_in(streams_of[4], 1), 0, NSHIFT - 1).astype(jnp.int32)
    channel_block_mask = place_ends((jax.random.randint(streams_of[5], (CHANNELS, SECTORS), 0, 4) < 3).astype(jnp.int32), jax.random.fold_in(streams_of[5], 1), 0, 1)
    block_size = place_ends(jax.random.randint(streams_of[6], (SECTORS,), B // 2, B + 1), jax.random.fold_in(streams_of[6], 1), B // 2, B).astype(jnp.int32)
    return dict(wavefunc=wavefunc, left_env=left_env, right_env=right_env, source=source, shift_class=shift_class, channel_block_mask=channel_block_mask, block_size=block_size)


def live_mask(block_size):
    positions = jnp.arange(B, dtype=jnp.int32)
    rows_live = positions[None, :, None] < block_size[:, None, None]
    cols_live = positions[None, None, :] < block_size[:, None, None]
    return jnp.logical_and(rows_live, cols_live).astype(jnp.float32)

def reference(wavefunc, left_env, right_env, source, shift_class, channel_block_mask, block_size):
    live = live_mask(block_size)
    masked = wavefunc * live

    def add_channel(total, items):
        left_single, right_single, kind, weight = items
        sources = jnp.take(source, kind, axis=0)
        block_tensors = jnp.take(masked, sources, axis=0)
        inner_product = jnp.einsum('lsk,lkz->lsz', left_single, block_tensors, precision=lax.Precision.HIGHEST)
        outer_product = jnp.einsum('mqh,mhr->mqr', inner_product, right_single, precision=lax.Precision.HIGHEST)
        return (total + outer_product * weight.astype(jnp.float32)[:, None, None], None)
    start = jnp.zeros((SECTORS, B, B), jnp.float32)
    total, unused = lax.scan(add_channel, start, (left_env, right_env, shift_class, channel_block_mask))
    return total * live / jnp.sqrt(jnp.float32(CHANNELS))
```

```python
import functools

import jax
import jax.numpy as jnp
from jax import lax
from jax.experimental import pallas as pl
from jax.experimental.pallas import tpu as pltpu
from jax.sharding import PartitionSpec as P

MESH = pl.DeviceIdType.MESH
STEPS = (1, 3, 2)


def split(value):
    high = value.astype(jnp.bfloat16)
    low = (value - high.astype(jnp.float32)).astype(jnp.bfloat16)
    return high, low


def product(a_high, a_low, b_high, b_low):
    dot = functools.partial(jnp.dot, preferred_element_type=jnp.float32)
    return dot(a_high, b_high) + dot(a_high, b_low) + dot(a_low, b_high)


def kernel(
    wave, left, right, source, shift, mask, size, out,
    gathered, left_f, right_f, left_h, left_l, right_h, right_l,
    part, got, mid, got2, source_s, shift_s, mask_s, size_s,
    local_sem, x1s, x1r, y1s, y1r, x2s, x2r, y2s, y2r, zs, zr, cs, cr,
    rs1, rr1, rs2, rr2,
):
    sector = lax.axis_index("sector")
    chan = lax.axis_index("chan")
    z, core = sector // 2, lax.rem(sector, 2)
    x, y = chan // 4, lax.rem(chan, 4)

    x_at = [lax.rem(x + d, 4) for d in range(4)]
    y_at = [lax.rem(y + d, 4) for d in range(4)]
    x_peer = {d: (sector, x_at[d] * 4 + y) for d in STEPS}
    y_peer = {d: (sector, x * 4 + y_at[d]) for d in STEPS}
    twin = (z * 2 + 1 - core, chan)
    near = (lax.rem(sector + 2 * core - 1 + 32, 32), chan)
    own, next_base = 4, 8 * core
    twin_there, near_there = 8 * core, 8 - 8 * core

    loads = [
        pltpu.make_async_copy(source, source_s, local_sem.at[0]),
        pltpu.make_async_copy(shift, shift_s, local_sem.at[1]),
        pltpu.make_async_copy(mask, mask_s, local_sem.at[2]),
        pltpu.make_async_copy(size, size_s, local_sem.at[3]),
        pltpu.make_async_copy(left, left_f, local_sem.at[4]),
        pltpu.make_async_copy(right, right_f, local_sem.at[5]),
    ]
    keep = pltpu.make_async_copy(wave, gathered.at[pl.ds(own, 4), x, y], local_sem.at[6])
    keep.start()

    barrier = pltpu.get_barrier_semaphore()
    partners = [x_peer[d] for d in STEPS] + [y_peer[d] for d in STEPS] + [twin, near]
    for partner in partners:
        pl.semaphore_signal(barrier, inc=1, device_id=partner, device_id_type=MESH)
    for load in loads:
        load.start()
    keep.wait()
    pl.semaphore_wait(barrier, len(partners))

    waits = []

    def send(view, there, send_sem, recv_sem, device):
        copy = pltpu.make_async_remote_copy(
            src_ref=view, dst_ref=there, send_sem=send_sem, recv_sem=recv_sem,
            device_id=device, device_id_type=MESH,
        )
        copy.start()
        waits.append(copy)
        return copy

    def first(q, base):
        a, b = {}, {}
        for d in STEPS:
            ref = gathered.at[pl.ds(base, 2), x, y]
            a[d] = send(ref, ref, x1s.at[q, d - 1], x1r.at[q, d - 1], x_peer[d])
            ref = gathered.at[pl.ds(base + 2, 2), x, y]
            b[d] = send(ref, ref, y1s.at[q, d - 1], y1r.at[q, d - 1], y_peer[d])
        return a, b

    def second(q, base, e):
        found = []
        for d in STEPS:
            ref = gathered.at[pl.ds(base, 2), x_at[(4 - e) % 4], y]
            a = send(ref, ref, y2s.at[q, e, d - 1], y2r.at[q, e, d - 1], y_peer[d])
            ref = gathered.at[pl.ds(base + 2, 2), x, y_at[(4 - e) % 4]]
            b = send(ref, ref, x2s.at[q, e, d - 1], x2r.at[q, e, d - 1], x_peer[d])
            found.append((d, a, b))
        return found

    o1 = first(0, own)
    ref = gathered.at[pl.ds(own, 4), x, y]
    over = send(ref, gathered.at[pl.ds(near_there, 4), x, y], zs.at[0], zr.at[0], near)
    o2 = {0: second(0, own, 0)}
    for d in STEPS:
        o1[0][d].wait_recv()
        o1[1][d].wait_recv()
        o2[d] = second(0, own, d)
    over.wait_recv()
    n1 = first(1, next_base)
    n2 = {0: second(1, next_base, 0)}
    for d in STEPS:
        n1[0][d].wait_recv()
        n1[1][d].wait_recv()
        n2[d] = second(1, next_base, d)

    twins = []

    def to_twin(i, first_block, blocks, at_x, at_y):
        ref = gathered.at[pl.ds(own + first_block, blocks), at_x, at_y]
        there = gathered.at[pl.ds(twin_there + first_block, blocks), at_x, at_y]
        twins.append(send(ref, there, cs.at[i], cr.at[i], twin))

    every = pl.ds(0, 4)
    to_twin(0, 0, 2, every, y)
    to_twin(1, 2, 2, x, every)
    for i, d in enumerate(STEPS):
        for e in (0,) + STEPS:
            for step, a, b in o2[e]:
                if step == d:
                    a.wait_recv()
                    b.wait_recv()
        to_twin(2 + 2 * i, 0, 2, every, y_at[4 - d])
        to_twin(3 + 2 * i, 2, 2, x_at[4 - d], every)

    for load in loads:
        load.wait()
    for w in range(2):
        for t in range(4):
            left_h[w, t], left_l[w, t] = split(left_f[w, t])
            right_h[w, t], right_l[w, t] = split(right_f[w, t])

    for e in (0,) + STEPS:
        for step, a, b in n2[e]:
            a.wait_recv()
            b.wait_recv()
    for copy in twins:
        copy.wait_recv()

    rows = lax.broadcasted_iota(jnp.int32, (256, 256), 0)
    cols = lax.broadcasted_iota(jnp.int32, (256, 256), 1)
    sums1 = []
    for t in range(4):
        target = sector * 4 + t
        total = None
        for w in range(2):
            channel = chan * 2 + w
            s = source_s[shift_s[channel], target]
            live = size_s[s] * mask_s[channel, target]
            place = jnp.clip(s - (sector * 4 - 4), 0, 11)
            block = gathered[place].reshape(256, 256)
            block = jnp.where(jnp.logical_and(rows < live, cols < live), block, 0.0)
            inner = product(left_h[w, t], left_l[w, t], *split(block))
            term = product(*split(inner), right_h[w, t], right_l[w, t])
            total = term if total is None else total + term
        part[0, t] = total[:, :128].reshape(4, 4, 16, 128)
        part[1, t] = total[:, 128:].reshape(4, 4, 16, 128)
        sent = []
        for d in STEPS:
            sent.append(send(part.at[0, t, x_at[d]], got.at[0, d - 1, t],
                             rs1.at[0, t, d - 1], rr1.at[0, t, d - 1], x_peer[d]))
            sent.append(send(part.at[1, t, every, y_at[d]], got.at[1, d - 1, t],
                             rs1.at[1, t, d - 1], rr1.at[1, t, d - 1], y_peer[d]))
        sums1.append(sent)

    sums2 = []
    for t in range(4):
        for copy in sums1[t]:
            copy.wait_recv()
        mid[0, t] = part[0, t, x] + got[0, 0, t] + got[0, 1, t] + got[0, 2, t]
        mid[1, t] = part[1, t, :, y] + got[1, 0, t] + got[1, 1, t] + got[1, 2, t]
        sent = []
        for d in STEPS:
            sent.append(send(mid.at[0, t, y_at[d]], got2.at[0, d - 1, t],
                             rs2.at[0, t, d - 1], rr2.at[0, t, d - 1], y_peer[d]))
            sent.append(send(mid.at[1, t, x_at[d]], got2.at[1, d - 1, t],
                             rs2.at[1, t, d - 1], rr2.at[1, t, d - 1], x_peer[d]))
        sums2.append(sent)

    row = lax.broadcasted_iota(jnp.int32, (16, 128), 0) + chan * 16
    col = lax.broadcasted_iota(jnp.int32, (16, 128), 1)
    scale = jnp.sqrt(jnp.float32(32))
    for t in range(4):
        for copy in sums2[t]:
            copy.wait_recv()
        live = size_s[sector * 4 + t]
        for half in range(2):
            at = y if half == 0 else x
            total = mid[half, t, at] + got2[half, 0, t] + got2[half, 1, t] + got2[half, 2, t]
            alive = jnp.logical_and(row < live, col + 128 * half < live)
            out[t, :, 128 * half:128 * (half + 1)] = jnp.where(alive, total, 0.0) / scale

    for copy in waits:
        copy.wait_send()


def body(wave, left, right, source, shift, mask, size):
    f32, bf16, i32 = jnp.float32, jnp.bfloat16, jnp.int32
    dma = pltpu.SemaphoreType.DMA
    return pl.pallas_call(
        kernel,
        out_shape=jax.ShapeDtypeStruct((4, 16, 256), f32),
        in_specs=[pl.BlockSpec(memory_space=pl.ANY)] * 7,
        out_specs=pl.BlockSpec(memory_space=pltpu.VMEM),
        scratch_shapes=[
            pltpu.VMEM((12, 4, 4, 16, 256), f32),
            pltpu.VMEM((2, 4, 256, 256), f32),
            pltpu.VMEM((2, 4, 256, 256), f32),
            pltpu.VMEM((2, 4, 256, 256), bf16),
            pltpu.VMEM((2, 4, 256, 256), bf16),
            pltpu.VMEM((2, 4, 256, 256), bf16),
            pltpu.VMEM((2, 4, 256, 256), bf16),
            pltpu.VMEM((2, 4, 4, 4, 16, 128), f32),
            pltpu.VMEM((2, 3, 4, 4, 16, 128), f32),
            pltpu.VMEM((2, 4, 4, 16, 128), f32),
            pltpu.VMEM((2, 3, 4, 16, 128), f32),
            pltpu.SMEM((5, 128), i32),
            pltpu.SMEM((32,), i32),
            pltpu.SMEM((32, 128), i32),
            pltpu.SMEM((128,), i32),
            dma((7,)),
            dma((2, 3)), dma((2, 3)), dma((2, 3)), dma((2, 3)),
            dma((2, 4, 3)), dma((2, 4, 3)), dma((2, 4, 3)), dma((2, 4, 3)),
            dma((1,)), dma((1,)), dma((8,)), dma((8,)),
            dma((2, 4, 3)), dma((2, 4, 3)), dma((2, 4, 3)), dma((2, 4, 3)),
        ],
        compiler_params=pltpu.CompilerParams(
            collective_id=0, has_side_effects=True, vmem_limit_bytes=40 * 2**20
        ),
        cost_estimate=pl.CostEstimate(
            flops=6 * 8 * 2 * 2 * 256**3 // 2, bytes_accessed=5 * 2**20, transcendentals=0
        ),
        name="heff",
    )(wave, left, right, source, shift, mask, size)


def solution(mesh):
    return jax.shard_map(
        body,
        mesh=mesh,
        in_specs=(
            P("sector", "chan", None),
            P("chan", "sector", None, None),
            P("chan", "sector", None, None),
            P(), P(), P(), P(),
        ),
        out_specs=P("sector", "chan", None),
        check_vma=False,
    )
```

```python
import functools

import jax
import jax.numpy as jnp
from jax import lax
from jax.experimental import pallas as pl
from jax.experimental.pallas import tpu as pltpu
from jax.sharding import PartitionSpec as P

MESH = pl.DeviceIdType.MESH
STEPS = (1, 3, 2)


def split(value):
    high = value.astype(jnp.bfloat16)
    low = (value - high.astype(jnp.float32)).astype(jnp.bfloat16)
    return high, low


def product(a_high, a_low, b_high, b_low):
    dot = functools.partial(jnp.dot, preferred_element_type=jnp.float32)
    return dot(a_high, b_high) + dot(a_high, b_low) + dot(a_low, b_high)


def kernel(
    wave, left, right, source, shift, mask, size, out,
    pair0, pair1, next0, next1, left_f, right_f, left_h, left_l, right_h, right_l,
    part0, part1, got, mid, got2, source_s, shift_s, mask_s, size_s,
    local_sem, s1, r1, s2, r2, zs, zr, n2s, n2r, twin_s, twin_r, near_s, near_r,
    ss1, sr1, ss2, sr2,
):
    sector = lax.axis_index("sector")
    chan = lax.axis_index("chan")
    z, core = sector // 2, lax.rem(sector, 2)
    x, y = chan // 4, lax.rem(chan, 4)

    x_at = [lax.rem(x + d, 4) for d in range(4)]
    y_at = [lax.rem(y + d, 4) for d in range(4)]
    x_peer = {d: (sector, x_at[d] * 4 + y) for d in STEPS}
    y_peer = {d: (sector, x * 4 + y_at[d]) for d in STEPS}
    twin = (z * 2 + 1 - core, chan)
    near = (lax.rem(sector + 2 * core - 1 + 32, 32), chan)
    targets = [3 - j + core * (2 * j - 3) for j in range(4)]
    kinds = (pair0.at[core], pair1.at[core])
    ends = (x_at, y_at)
    starts = (y_at, x_at)
    first_peer = (x_peer, y_peer)
    second_peer = (y_peer, x_peer)
    mine = [wave.at[pl.ds(2 * core, 2)], wave.at[pl.ds(2 - 2 * core, 2)]]

    loads = [
        pltpu.make_async_copy(source, source_s, local_sem.at[0]),
        pltpu.make_async_copy(shift, shift_s, local_sem.at[1]),
        pltpu.make_async_copy(mask, mask_s, local_sem.at[2]),
        pltpu.make_async_copy(size, size_s, local_sem.at[3]),
    ]
    left_load = pltpu.make_async_copy(left, left_f, local_sem.at[4])
    right_load = pltpu.make_async_copy(right, right_f, local_sem.at[5])
    keeps = [
        pltpu.make_async_copy(mine[0], pair0.at[core, y, x], local_sem.at[6]),
        pltpu.make_async_copy(mine[1], pair1.at[core, x, y], local_sem.at[7]),
    ]
    for keep in keeps:
        keep.start()

    barrier = pltpu.get_barrier_semaphore()
    partners = [x_peer[d] for d in STEPS] + [y_peer[d] for d in STEPS] + [twin]
    inner_sector = jnp.logical_and(sector > 0, sector < 31)

    @pl.when(inner_sector)
    def _():
        pl.semaphore_signal(barrier, inc=1, device_id=near, device_id_type=MESH)

    for partner in partners:
        pl.semaphore_signal(barrier, inc=1, device_id=partner, device_id_type=MESH)
    pl.semaphore_wait(barrier, len(partners) + inner_sector.astype(jnp.int32))

    sent, sent_near = [], []

    def planned(view, there, send_sem, recv_sem, device):
        return pltpu.make_async_remote_copy(
            src_ref=view, dst_ref=there, send_sem=send_sem, recv_sem=recv_sem,
            device_id=device, device_id_type=MESH,
        )

    def send(*where):
        copy = planned(*where)
        copy.start()
        sent.append(copy)
        return copy

    def send_near(copies):
        @pl.when(inner_sector)
        def _():
            for copy in copies:
                copy.start()

        sent_near.extend(copies)
        return copies

    def wait_near(copies):
        @pl.when(inner_sector)
        def _():
            for copy in copies:
                copy.wait_recv()

    first = {}
    for d in STEPS:
        for kind in range(2):
            first[kind, d] = send(
                mine[kind], kinds[kind].at[starts[kind][0], ends[kind][0]],
                s1.at[kind, d - 1], r1.at[kind, d - 1], first_peer[kind][d])

    nexts = (next0, next1)
    second, over, second_n = {}, {}, {}

    def piece(refs, kind, e):
        return refs[kind].at[starts[kind][0], ends[kind][(4 - e) % 4]]

    def pass_on(kind, e):
        here = piece(kinds, kind, e)
        for d in (2, 1, 3):
            second[kind, e, d] = send(
                here if e else mine[kind], here,
                s2.at[kind, e, d - 1], r2.at[kind, e, d - 1], second_peer[kind][d])

    def cross(kind, e):
        over[kind, e] = planned(piece(kinds, kind, e) if e else mine[kind], piece(nexts, kind, e),
                                zs.at[kind, e], zr.at[kind, e], near)
        send_near([over[kind, e]])

    def pass_on_n(e):
        for kind in range(2):
            here = piece(nexts, kind, e)
            for d in (1, 3):
                second_n[kind, e, d] = planned(
                    here, here, n2s.at[kind, e, d // 2], n2r.at[kind, e, d // 2],
                    second_peer[kind][d])
        copies = [second_n[kind, e, d] for kind in range(2) for d in (1, 3)]

        @pl.when(inner_sector)
        def _():
            for kind in range(2):
                over[kind, e].wait_recv()
                for d in (1, 3):
                    second_n[kind, e, d].start()

        sent_near.extend(copies)

    twins, groups = [], {}

    def group(kind, d):
        at = starts[kind][(4 - d) % 4]
        ref = kinds[kind].at[at]
        if d == 2:
            groups[kind] = planned(
                ref, nexts[kind].at[at], near_s.at[kind], near_r.at[kind], near)
            send_near([groups[kind]])
        twins.append(send(ref, ref, twin_s.at[kind, d], twin_r.at[kind, d], twin))

    for kind in range(2):
        cross(kind, 0)
    for kind in range(2):
        pass_on(kind, 0)
    for load in loads:
        load.start()
    left_load.start()
    right_load.start()
    for d in STEPS:
        for kind in range(2):
            first[kind, d].wait_recv()
            cross(kind, d)
            pass_on(kind, d)
    for keep in keeps:
        keep.wait()
    for kind in range(2):
        group(kind, 0)
    left_load.wait()
    for w in range(2):
        for t in range(4):
            left_h[w, t], left_l[w, t] = split(left_f[w, t])
    for e in (0,) + STEPS:
        pass_on_n(e)
    for d in (2, 1, 3):
        for kind in range(2):
            for e in range(4):
                second[kind, e, d].wait_recv()
            group(kind, d)
        if d == 2:
            right_load.wait()
            for w in range(2):
                for t in range(4):
                    right_h[w, t], right_l[w, t] = split(right_f[w, t])
    for load in loads:
        load.wait()
    for copy in twins:
        copy.wait_recv()

    def assembled(ref, swapped):
        return jnp.concatenate(
            [ref(b, a) if swapped else ref(a, b) for a in range(4) for b in range(4)], axis=0)

    rows = lax.broadcasted_iota(jnp.int32, (256, 256), 0)
    cols = lax.broadcasted_iota(jnp.int32, (256, 256), 1)
    sums1 = []
    for j in range(4):
        if j % 2 == 0:
            kind = j // 2
            wait_near([groups[kind]] + [second_n[kind, e, d] for e in range(4) for d in (1, 3)])
        target = sector * 4 + targets[j]
        total = None
        for w in range(2):
            channel = chan * 2 + w
            s = source_s[shift_s[channel], target]
            live = size_s[s] * mask_s[channel, target]
            place = s - z * 8
            at = jnp.clip(place, 0, 7)
            owner, i, upper = at // 4, lax.rem(at, 2), lax.rem(at, 4) // 2
            block = jnp.where(
                upper == owner,
                assembled(lambda a, b: pair0[owner, a, b, i], True),
                assembled(lambda a, b: pair1[owner, a, b, i], False))
            for i in range(2):
                block = jnp.where(place == i - 2 + 10 * core,
                                  assembled(lambda a, b: next0[a, b, i], True), block)
            if j >= 2:
                for i in range(2):
                    block = jnp.where(place == i - 4 + 14 * core,
                                      assembled(lambda a, b: next1[a, b, i], False), block)
            block = jnp.where(jnp.logical_and(rows < live, cols < live), block, 0.0)
            inner = product(left_h[w, targets[j]], left_l[w, targets[j]], *split(block))
            term = product(*split(inner), right_h[w, targets[j]], right_l[w, targets[j]])
            total = term if total is None else total + term
        for a in range(4):
            for b in range(4):
                r = 64 * a + 16 * b
                part0[j, a, b] = total[r:r + 16, :128]
                part1[j, b, a] = total[r:r + 16, 128:]
        step = []
        for d in STEPS:
            step.append(send(part0.at[j, x_at[d]], got.at[0, d - 1, j],
                             ss1.at[0, j, d - 1], sr1.at[0, j, d - 1], x_peer[d]))
            step.append(send(part1.at[j, y_at[d]], got.at[1, d - 1, j],
                             ss1.at[1, j, d - 1], sr1.at[1, j, d - 1], y_peer[d]))
        sums1.append(step)

    sums2 = []
    for j in range(4):
        for copy in sums1[j]:
            copy.wait_recv()
        mid[0, j] = part0[j, x] + got[0, 0, j] + got[0, 1, j] + got[0, 2, j]
        mid[1, j] = part1[j, y] + got[1, 0, j] + got[1, 1, j] + got[1, 2, j]
        step = []
        for d in STEPS:
            step.append(send(mid.at[0, j, y_at[d]], got2.at[0, d - 1, j],
                             ss2.at[0, j, d - 1], sr2.at[0, j, d - 1], y_peer[d]))
            step.append(send(mid.at[1, j, x_at[d]], got2.at[1, d - 1, j],
                             ss2.at[1, j, d - 1], sr2.at[1, j, d - 1], x_peer[d]))
        sums2.append(step)

    row = lax.broadcasted_iota(jnp.int32, (16, 128), 0) + chan * 16
    col = lax.broadcasted_iota(jnp.int32, (16, 128), 1)
    scale = jnp.sqrt(jnp.float32(32))
    for j in range(4):
        for copy in sums2[j]:
            copy.wait_recv()
        live = size_s[sector * 4 + targets[j]]
        for half, at in ((0, y), (1, x)):
            total = mid[half, j, at] + got2[half, 0, j] + got2[half, 1, j] + got2[half, 2, j]
            alive = jnp.logical_and(row < live, col + 128 * half < live)
            out[targets[j], :, 128 * half:128 * (half + 1)] = jnp.where(alive, total, 0.0) / scale

    for copy in sent:
        copy.wait_send()

    @pl.when(inner_sector)
    def _():
        for copy in sent_near:
            copy.wait_send()


def body(wave, left, right, source, shift, mask, size):
    f32, bf16, i32 = jnp.float32, jnp.bfloat16, jnp.int32
    dma = pltpu.SemaphoreType.DMA
    return pl.pallas_call(
        kernel,
        out_shape=jax.ShapeDtypeStruct((4, 16, 256), f32),
        in_specs=[pl.BlockSpec(memory_space=pl.ANY)] * 7,
        out_specs=pl.BlockSpec(memory_space=pltpu.VMEM),
        scratch_shapes=[
            pltpu.VMEM((2, 4, 4, 2, 16, 256), f32),
            pltpu.VMEM((2, 4, 4, 2, 16, 256), f32),
            pltpu.VMEM((4, 4, 2, 16, 256), f32),
            pltpu.VMEM((4, 4, 2, 16, 256), f32),
            pltpu.VMEM((2, 4, 256, 256), f32),
            pltpu.VMEM((2, 4, 256, 256), f32),
            pltpu.VMEM((2, 4, 256, 256), bf16),
            pltpu.VMEM((2, 4, 256, 256), bf16),
            pltpu.VMEM((2, 4, 256, 256), bf16),
            pltpu.VMEM((2, 4, 256, 256), bf16),
            pltpu.VMEM((4, 4, 4, 16, 128), f32),
            pltpu.VMEM((4, 4, 4, 16, 128), f32),
            pltpu.VMEM((2, 3, 4, 4, 16, 128), f32),
            pltpu.VMEM((2, 4, 4, 16, 128), f32),
            pltpu.VMEM((2, 3, 4, 16, 128), f32),
            pltpu.SMEM((5, 128), i32),
            pltpu.SMEM((32,), i32),
            pltpu.SMEM((32, 128), i32),
            pltpu.SMEM((128,), i32),
            dma((8,)),
            dma((2, 3)), dma((2, 3)), dma((2, 4, 3)), dma((2, 4, 3)),
            dma((2, 4)), dma((2, 4)), dma((2, 4, 2)), dma((2, 4, 2)),
            dma((2, 4)), dma((2, 4)), dma((2,)), dma((2,)),
            dma((2, 4, 3)), dma((2, 4, 3)), dma((2, 4, 3)), dma((2, 4, 3)),
        ],
        compiler_params=pltpu.CompilerParams(
            collective_id=0, has_side_effects=True, vmem_limit_bytes=60 * 2**20
        ),
        cost_estimate=pl.CostEstimate(
            flops=3 * 8 * 2 * 2 * 256**3, bytes_accessed=5 * 2**20, transcendentals=0
        ),
        name="heff",
    )(wave, left, right, source, shift, mask, size)


def solution(mesh):
    return jax.shard_map(
        body,
        mesh=mesh,
        in_specs=(
            P("sector", "chan", None),
            P("chan", "sector", None, None),
            P("chan", "sector", None, None),
            P(), P(), P(), P(),
        ),
        out_specs=P("sector", "chan", None),
        check_vma=False,
    )
```

```python
import functools

import jax
import jax.numpy as jnp
from jax import lax
from jax.experimental import pallas as pl
from jax.experimental.pallas import tpu as pltpu
from jax.sharding import PartitionSpec as P

MESH = pl.DeviceIdType.MESH
STEPS = (1, 3, 2)


def split(value):
    high = value.astype(jnp.bfloat16)
    low = (value - high.astype(jnp.float32)).astype(jnp.bfloat16)
    return high, low


def product(a_high, a_low, b_high, b_low):
    dot = functools.partial(jnp.dot, preferred_element_type=jnp.float32)
    return dot(a_high, b_high) + dot(a_high, b_low) + dot(a_low, b_high)


def kernel(
    wave, left, right, source, shift, mask, size, out,
    pair0, pair1, next0, next1, left_f, right_f, left_h, left_l, right_h, right_l,
    part0, part1, got, mid, got2, source_s, shift_s, mask_s, size_s,
    local_sem, s1, r1, s2, r2, zs, zr, n2s, n2r, twin_s, twin_r, near_s, near_r,
    ss1, sr1, ss2, sr2,
):
    sector = lax.axis_index("sector")
    chan = lax.axis_index("chan")
    z, core = sector // 2, lax.rem(sector, 2)
    x, y = chan // 4, lax.rem(chan, 4)

    x_at = [lax.rem(x + d, 4) for d in range(4)]
    y_at = [lax.rem(y + d, 4) for d in range(4)]
    x_peer = {d: (sector, x_at[d] * 4 + y) for d in STEPS}
    y_peer = {d: (sector, x * 4 + y_at[d]) for d in STEPS}
    twin = (z * 2 + 1 - core, chan)
    near = (lax.rem(sector + 2 * core - 1 + 32, 32), chan)
    targets = [3 - j + core * (2 * j - 3) for j in range(4)]
    kinds = (pair0.at[core], pair1.at[core])
    ends = (x_at, y_at)
    starts = (y_at, x_at)
    first_peer = (x_peer, y_peer)
    second_peer = (y_peer, x_peer)
    mine = [wave.at[pl.ds(2 * core, 2)], wave.at[pl.ds(2 - 2 * core, 2)]]

    loads = [
        pltpu.make_async_copy(source, source_s, local_sem.at[0]),
        pltpu.make_async_copy(shift, shift_s, local_sem.at[1]),
        pltpu.make_async_copy(mask, mask_s, local_sem.at[2]),
        pltpu.make_async_copy(size, size_s, local_sem.at[3]),
    ]
    left_load = pltpu.make_async_copy(left, left_f, local_sem.at[4])
    right_load = pltpu.make_async_copy(right, right_f, local_sem.at[5])
    keeps = [
        pltpu.make_async_copy(mine[0], pair0.at[core, y, x], local_sem.at[6]),
        pltpu.make_async_copy(mine[1], pair1.at[core, x, y], local_sem.at[7]),
    ]
    for keep in keeps:
        keep.start()
    left_load.start()
    right_load.start()
    for load in loads:
        load.start()

    barrier = pltpu.get_barrier_semaphore()
    partners = [x_peer[d] for d in STEPS] + [y_peer[d] for d in STEPS] + [twin]
    inner_sector = jnp.logical_and(sector > 0, sector < 31)

    @pl.when(inner_sector)
    def _():
        pl.semaphore_signal(barrier, inc=1, device_id=near, device_id_type=MESH)

    for partner in partners:
        pl.semaphore_signal(barrier, inc=1, device_id=partner, device_id_type=MESH)
    pl.semaphore_wait(barrier, len(partners) + inner_sector.astype(jnp.int32))

    sent, sent_near = [], []

    def planned(view, there, send_sem, recv_sem, device):
        return pltpu.make_async_remote_copy(
            src_ref=view, dst_ref=there, send_sem=send_sem, recv_sem=recv_sem,
            device_id=device, device_id_type=MESH,
        )

    def send(*where):
        copy = planned(*where)
        copy.start()
        sent.append(copy)
        return copy

    def send_near(copies):
        @pl.when(inner_sector)
        def _():
            for copy in copies:
                copy.start()

        sent_near.extend(copies)
        return copies

    def wait_near(copies):
        @pl.when(inner_sector)
        def _():
            for copy in copies:
                copy.wait_recv()

    first = {}
    for d in STEPS:
        for kind in range(2):
            first[kind, d] = send(
                mine[kind], kinds[kind].at[starts[kind][0], ends[kind][0]],
                s1.at[kind, d - 1], r1.at[kind, d - 1], first_peer[kind][d])

    nexts = (next0, next1)
    second, over, second_n = {}, {}, {}

    def piece(refs, kind, e):
        return refs[kind].at[starts[kind][0], ends[kind][(4 - e) % 4]]

    def pass_on(kind, e):
        here = piece(kinds, kind, e)
        for d in (2, 1, 3):
            second[kind, e, d] = send(
                here if e else mine[kind], here,
                s2.at[kind, e, d - 1], r2.at[kind, e, d - 1], second_peer[kind][d])

    def cross(kind, e):
        over[kind, e] = planned(piece(kinds, kind, e) if e else mine[kind], piece(nexts, kind, e),
                                zs.at[kind, e], zr.at[kind, e], near)
        send_near([over[kind, e]])

    def pass_on_n(e):
        for kind in range(2):
            here = piece(nexts, kind, e)
            for d in (1, 3):
                second_n[kind, e, d] = planned(
                    here, here, n2s.at[kind, e, d // 2], n2r.at[kind, e, d // 2],
                    second_peer[kind][d])
        copies = [second_n[kind, e, d] for kind in range(2) for d in (1, 3)]

        @pl.when(inner_sector)
        def _():
            for kind in range(2):
                over[kind, e].wait_recv()
                for d in (1, 3):
                    second_n[kind, e, d].start()

        sent_near.extend(copies)

    twins, groups = [], {}

    def group(kind, d):
        at = starts[kind][(4 - d) % 4]
        ref = kinds[kind].at[at]
        if d == 2:
            groups[kind] = planned(
                ref, nexts[kind].at[at], near_s.at[kind], near_r.at[kind], near)
            send_near([groups[kind]])
        twins.append(send(ref, ref, twin_s.at[kind, d], twin_r.at[kind, d], twin))

    for kind in range(2):
        cross(kind, 0)
    for kind in range(2):
        pass_on(kind, 0)
    left_load.wait()
    for w in range(2):
        for t in range(4):
            left_h[w, t], left_l[w, t] = split(left_f[w, t])
    right_load.wait()
    for w in range(2):
        for t in range(4):
            right_h[w, t], right_l[w, t] = split(right_f[w, t])
    for d in STEPS:
        for kind in range(2):
            first[kind, d].wait_recv()
            cross(kind, d)
            pass_on(kind, d)
    for keep in keeps:
        keep.wait()
    for kind in range(2):
        group(kind, 0)
    for e in (0,) + STEPS:
        pass_on_n(e)
    for d in (2, 1, 3):
        for kind in range(2):
            for e in range(4):
                second[kind, e, d].wait_recv()
            group(kind, d)
    for load in loads:
        load.wait()
    for copy in twins:
        copy.wait_recv()

    def assembled(ref, swapped):
        return jnp.concatenate(
            [ref(b, a) if swapped else ref(a, b) for a in range(4) for b in range(4)], axis=0)

    rows = lax.broadcasted_iota(jnp.int32, (256, 256), 0)
    cols = lax.broadcasted_iota(jnp.int32, (256, 256), 1)
    sums1 = []
    for j in range(4):
        if j % 2 == 0:
            kind = j // 2
            wait_near([groups[kind]] + [second_n[kind, e, d] for e in range(4) for d in (1, 3)])
        target = sector * 4 + targets[j]
        total = None
        for w in range(2):
            channel = chan * 2 + w
            s = source_s[shift_s[channel], target]
            live = size_s[s] * mask_s[channel, target]
            place = s - z * 8
            at = jnp.clip(place, 0, 7)
            owner, i, upper = at // 4, lax.rem(at, 2), lax.rem(at, 4) // 2
            block = jnp.where(
                upper == owner,
                assembled(lambda a, b: pair0[owner, a, b, i], True),
                assembled(lambda a, b: pair1[owner, a, b, i], False))
            for i in range(2):
                block = jnp.where(place == i - 2 + 10 * core,
                                  assembled(lambda a, b: next0[a, b, i], True), block)
            if j >= 2:
                for i in range(2):
                    block = jnp.where(place == i - 4 + 14 * core,
                                      assembled(lambda a, b: next1[a, b, i], False), block)
            block = jnp.where(jnp.logical_and(rows < live, cols < live), block, 0.0)
            inner = product(left_h[w, targets[j]], left_l[w, targets[j]], *split(block))
            term = product(*split(inner), right_h[w, targets[j]], right_l[w, targets[j]])
            total = term if total is None else total + term
        for a in range(4):
            for b in range(4):
                r = 64 * a + 16 * b
                part0[j, a, b] = total[r:r + 16, :128]
                part1[j, b, a] = total[r:r + 16, 128:]
        step = []
        for d in STEPS:
            step.append(send(part0.at[j, x_at[d]], got.at[0, d - 1, j],
                             ss1.at[0, j, d - 1], sr1.at[0, j, d - 1], x_peer[d]))
            step.append(send(part1.at[j, y_at[d]], got.at[1, d - 1, j],
                             ss1.at[1, j, d - 1], sr1.at[1, j, d - 1], y_peer[d]))
        sums1.append(step)

    sums2 = []
    for j in range(4):
        for copy in sums1[j]:
            copy.wait_recv()
        mid[0, j] = part0[j, x] + got[0, 0, j] + got[0, 1, j] + got[0, 2, j]
        mid[1, j] = part1[j, y] + got[1, 0, j] + got[1, 1, j] + got[1, 2, j]
        step = []
        for d in STEPS:
            step.append(send(mid.at[0, j, y_at[d]], got2.at[0, d - 1, j],
                             ss2.at[0, j, d - 1], sr2.at[0, j, d - 1], y_peer[d]))
            step.append(send(mid.at[1, j, x_at[d]], got2.at[1, d - 1, j],
                             ss2.at[1, j, d - 1], sr2.at[1, j, d - 1], x_peer[d]))
        sums2.append(step)

    row = lax.broadcasted_iota(jnp.int32, (16, 128), 0) + chan * 16
    col = lax.broadcasted_iota(jnp.int32, (16, 128), 1)
    scale = jnp.sqrt(jnp.float32(32))
    for j in range(4):
        for copy in sums2[j]:
            copy.wait_recv()
        live = size_s[sector * 4 + targets[j]]
        for half, at in ((0, y), (1, x)):
            total = mid[half, j, at] + got2[half, 0, j] + got2[half, 1, j] + got2[half, 2, j]
            alive = jnp.logical_and(row < live, col + 128 * half < live)
            out[targets[j], :, 128 * half:128 * (half + 1)] = jnp.where(alive, total, 0.0) / scale

    for copy in sent:
        copy.wait_send()

    @pl.when(inner_sector)
    def _():
        for copy in sent_near:
            copy.wait_send()


def body(wave, left, right, source, shift, mask, size):
    f32, bf16, i32 = jnp.float32, jnp.bfloat16, jnp.int32
    dma = pltpu.SemaphoreType.DMA
    return pl.pallas_call(
        kernel,
        out_shape=jax.ShapeDtypeStruct((4, 16, 256), f32),
        in_specs=[pl.BlockSpec(memory_space=pl.ANY)] * 7,
        out_specs=pl.BlockSpec(memory_space=pltpu.VMEM),
        scratch_shapes=[
            pltpu.VMEM((2, 4, 4, 2, 16, 256), f32),
            pltpu.VMEM((2, 4, 4, 2, 16, 256), f32),
            pltpu.VMEM((4, 4, 2, 16, 256), f32),
            pltpu.VMEM((4, 4, 2, 16, 256), f32),
            pltpu.VMEM((2, 4, 256, 256), f32),
            pltpu.VMEM((2, 4, 256, 256), f32),
            pltpu.VMEM((2, 4, 256, 256), bf16),
            pltpu.VMEM((2, 4, 256, 256), bf16),
            pltpu.VMEM((2, 4, 256, 256), bf16),
            pltpu.VMEM((2, 4, 256, 256), bf16),
            pltpu.VMEM((4, 4, 4, 16, 128), f32),
            pltpu.VMEM((4, 4, 4, 16, 128), f32),
            pltpu.VMEM((2, 3, 4, 4, 16, 128), f32),
            pltpu.VMEM((2, 4, 4, 16, 128), f32),
            pltpu.VMEM((2, 3, 4, 16, 128), f32),
            pltpu.SMEM((5, 128), i32),
            pltpu.SMEM((32,), i32),
            pltpu.SMEM((32, 128), i32),
            pltpu.SMEM((128,), i32),
            dma((8,)),
            dma((2, 3)), dma((2, 3)), dma((2, 4, 3)), dma((2, 4, 3)),
            dma((2, 4)), dma((2, 4)), dma((2, 4, 2)), dma((2, 4, 2)),
            dma((2, 4)), dma((2, 4)), dma((2,)), dma((2,)),
            dma((2, 4, 3)), dma((2, 4, 3)), dma((2, 4, 3)), dma((2, 4, 3)),
        ],
        compiler_params=pltpu.CompilerParams(
            collective_id=0, has_side_effects=True, vmem_limit_bytes=53 * 2**20
        ),
        cost_estimate=pl.CostEstimate(
            flops=3 * 8 * 2 * 2 * 256**3, bytes_accessed=5 * 2**20, transcendentals=0
        ),
        name="heff",
    )(*[pltpu.with_memory_space_constraint(v, pltpu.HBM) for v in (wave, left, right, source, shift, mask, size)])


def solution(mesh):
    return jax.shard_map(
        body,
        mesh=mesh,
        in_specs=(
            P("sector", "chan", None),
            P("chan", "sector", None, None),
            P("chan", "sector", None, None),
            P(), P(), P(), P(),
        ),
        out_specs=P("sector", "chan", None),
        check_vma=False,
    )
```

```python
import functools

import jax
import jax.numpy as jnp
from jax import lax
from jax.experimental import pallas as pl
from jax.experimental.pallas import tpu as pltpu
from jax.sharding import PartitionSpec as P

MESH = pl.DeviceIdType.MESH
STEPS = (1, 3, 2)


def split(value):
    high = value.astype(jnp.bfloat16)
    low = (value - high.astype(jnp.float32)).astype(jnp.bfloat16)
    return high, low


def product(a_high, a_low, b_high, b_low):
    dot = functools.partial(jnp.dot, preferred_element_type=jnp.float32)
    return dot(a_high, b_high) + dot(a_high, b_low) + dot(a_low, b_high)


def kernel(
    wave, left, right, source, shift, mask, size, out,
    pair0, pair1, next0, next1, left_f, right_f, left_h, left_l, right_h, right_l,
    part0, part1, got, mid, got2, source_s, shift_s, mask_s, size_s,
    local_sem, s1, r1, s2, r2, zs, zr, n2s, n2r, twin_s, twin_r, near_s, near_r,
    ss1, sr1, ss2, sr2,
):
    sector = lax.axis_index("sector")
    chan = lax.axis_index("chan")
    z, core = sector // 2, lax.rem(sector, 2)
    x, y = chan // 4, lax.rem(chan, 4)

    x_at = [lax.rem(x + d, 4) for d in range(4)]
    y_at = [lax.rem(y + d, 4) for d in range(4)]
    x_peer = {d: (sector, x_at[d] * 4 + y) for d in STEPS}
    y_peer = {d: (sector, x * 4 + y_at[d]) for d in STEPS}
    twin = (z * 2 + 1 - core, chan)
    near = (lax.rem(sector + 2 * core - 1 + 32, 32), chan)
    targets = [3 - j + core * (2 * j - 3) for j in range(4)]
    kinds = (pair0.at[core], pair1.at[core])
    ends = (x_at, y_at)
    starts = (y_at, x_at)
    first_peer = (x_peer, y_peer)
    second_peer = (y_peer, x_peer)
    home = [wave.at[pl.ds(2 * core, 2)], wave.at[pl.ds(2 - 2 * core, 2)]]

    loads = [
        pltpu.make_async_copy(source, source_s, local_sem.at[0]),
        pltpu.make_async_copy(shift, shift_s, local_sem.at[1]),
        pltpu.make_async_copy(mask, mask_s, local_sem.at[2]),
        pltpu.make_async_copy(size, size_s, local_sem.at[3]),
    ]
    left_load = pltpu.make_async_copy(left, left_f, local_sem.at[4])
    right_load = pltpu.make_async_copy(right, right_f, local_sem.at[5])
    keeps = [
        pltpu.make_async_copy(home[0], pair0.at[core, y, x], local_sem.at[6]),
        pltpu.make_async_copy(home[1], pair1.at[core, x, y], local_sem.at[7]),
    ]
    for keep in keeps:
        keep.start()

    mine = [pair0.at[core, y, x], pair1.at[core, x, y]]
    barrier = pltpu.get_barrier_semaphore()
    partners = [x_peer[d] for d in STEPS] + [y_peer[d] for d in STEPS] + [twin]
    inner_sector = jnp.logical_and(sector > 0, sector < 31)

    @pl.when(inner_sector)
    def _():
        pl.semaphore_signal(barrier, inc=1, device_id=near, device_id_type=MESH)

    for partner in partners:
        pl.semaphore_signal(barrier, inc=1, device_id=partner, device_id_type=MESH)
    for keep in keeps:
        keep.wait()
    pl.semaphore_wait(barrier, len(partners) + inner_sector.astype(jnp.int32))

    sent, sent_near = [], []

    def planned(view, there, send_sem, recv_sem, device):
        return pltpu.make_async_remote_copy(
            src_ref=view, dst_ref=there, send_sem=send_sem, recv_sem=recv_sem,
            device_id=device, device_id_type=MESH,
        )

    def send(*where):
        copy = planned(*where)
        copy.start()
        sent.append(copy)
        return copy

    def send_near(copies):
        @pl.when(inner_sector)
        def _():
            for copy in copies:
                copy.start()

        sent_near.extend(copies)
        return copies

    def wait_near(copies):
        @pl.when(inner_sector)
        def _():
            for copy in copies:
                copy.wait_recv()

    first = {}
    for d in STEPS:
        for kind in range(2):
            first[kind, d] = send(
                mine[kind], kinds[kind].at[starts[kind][0], ends[kind][0]],
                s1.at[kind, d - 1], r1.at[kind, d - 1], first_peer[kind][d])

    nexts = (next0, next1)
    second, over, second_n = {}, {}, {}

    def piece(refs, kind, e):
        return refs[kind].at[starts[kind][0], ends[kind][(4 - e) % 4]]

    def pass_on(kind, e):
        here = piece(kinds, kind, e)
        for d in (2, 1, 3):
            second[kind, e, d] = send(
                here if e else mine[kind], here,
                s2.at[kind, e, d - 1], r2.at[kind, e, d - 1], second_peer[kind][d])

    def cross(kind, e):
        over[kind, e] = planned(piece(kinds, kind, e) if e else mine[kind], piece(nexts, kind, e),
                                zs.at[kind, e], zr.at[kind, e], near)
        send_near([over[kind, e]])

    def pass_on_n(e):
        for kind in range(2):
            here = piece(nexts, kind, e)
            for d in (1, 3):
                second_n[kind, e, d] = planned(
                    here, here, n2s.at[kind, e, d // 2], n2r.at[kind, e, d // 2],
                    second_peer[kind][d])
        copies = [second_n[kind, e, d] for kind in range(2) for d in (1, 3)]

        @pl.when(inner_sector)
        def _():
            for kind in range(2):
                over[kind, e].wait_recv()
                for d in (1, 3):
                    second_n[kind, e, d].start()

        sent_near.extend(copies)

    twins, groups = [], {}

    def group(kind, d):
        at = starts[kind][(4 - d) % 4]
        ref = kinds[kind].at[at]
        if d == 2:
            groups[kind] = planned(
                ref, nexts[kind].at[at], near_s.at[kind], near_r.at[kind], near)
            send_near([groups[kind]])
        twins.append(send(ref, ref, twin_s.at[kind, d], twin_r.at[kind, d], twin))

    for kind in range(2):
        cross(kind, 0)
    for kind in range(2):
        pass_on(kind, 0)
    left_load.start()
    right_load.start()
    for load in loads:
        load.start()
    left_load.wait()
    for w in range(2):
        for t in range(4):
            left_h[w, t], left_l[w, t] = split(left_f[w, t])
    right_load.wait()
    for w in range(2):
        for t in range(4):
            right_h[w, t], right_l[w, t] = split(right_f[w, t])
    for d in STEPS:
        for kind in range(2):
            first[kind, d].wait_recv()
            cross(kind, d)
            pass_on(kind, d)
    for kind in range(2):
        group(kind, 0)
    for e in (0,) + STEPS:
        pass_on_n(e)
    for d in (2, 1, 3):
        for kind in range(2):
            for e in range(4):
                second[kind, e, d].wait_recv()
            group(kind, d)
    for load in loads:
        load.wait()
    for copy in twins:
        copy.wait_recv()

    def assembled(ref, swapped):
        return jnp.concatenate(
            [ref(b, a) if swapped else ref(a, b) for a in range(4) for b in range(4)], axis=0)

    rows = lax.broadcasted_iota(jnp.int32, (256, 256), 0)
    cols = lax.broadcasted_iota(jnp.int32, (256, 256), 1)
    sums1 = []
    for j in range(4):
        if j % 2 == 0:
            kind = j // 2
            wait_near([groups[kind]] + [second_n[kind, e, d] for e in range(4) for d in (1, 3)])
        target = sector * 4 + targets[j]
        total = None
        for w in range(2):
            channel = chan * 2 + w
            s = source_s[shift_s[channel], target]
            live = size_s[s] * mask_s[channel, target]
            place = s - z * 8
            at = jnp.clip(place, 0, 7)
            owner, i, upper = at // 4, lax.rem(at, 2), lax.rem(at, 4) // 2
            block = jnp.where(
                upper == owner,
                assembled(lambda a, b: pair0[owner, a, b, i], True),
                assembled(lambda a, b: pair1[owner, a, b, i], False))
            for i in range(2):
                block = jnp.where(place == i - 2 + 10 * core,
                                  assembled(lambda a, b: next0[a, b, i], True), block)
            if j >= 2:
                for i in range(2):
                    block = jnp.where(place == i - 4 + 14 * core,
                                      assembled(lambda a, b: next1[a, b, i], False), block)
            block = jnp.where(jnp.logical_and(rows < live, cols < live), block, 0.0)
            inner = product(left_h[w, targets[j]], left_l[w, targets[j]], *split(block))
            term = product(*split(inner), right_h[w, targets[j]], right_l[w, targets[j]])
            total = term if total is None else total + term
        for a in range(4):
            for b in range(4):
                r = 64 * a + 16 * b
                part0[j, a, b] = total[r:r + 16, :128]
                part1[j, b, a] = total[r:r + 16, 128:]
        step = []
        for d in (2, 1, 3):
            step.append(send(part0.at[j, x_at[d]], got.at[0, d - 1, j],
                             ss1.at[0, j, d - 1], sr1.at[0, j, d - 1], x_peer[d]))
            step.append(send(part1.at[j, y_at[d]], got.at[1, d - 1, j],
                             ss1.at[1, j, d - 1], sr1.at[1, j, d - 1], y_peer[d]))
        sums1.append(step)

    sums2 = []
    for j in range(4):
        step = []
        for copy in sums1[j][0::2]:
            copy.wait_recv()
        mid[0, j] = part0[j, x] + got[0, 0, j] + got[0, 1, j] + got[0, 2, j]
        for d in (2, 1, 3):
            step.append(send(mid.at[0, j, y_at[d]], got2.at[0, d - 1, j],
                             ss2.at[0, j, d - 1], sr2.at[0, j, d - 1], y_peer[d]))
        for copy in sums1[j][1::2]:
            copy.wait_recv()
        mid[1, j] = part1[j, y] + got[1, 0, j] + got[1, 1, j] + got[1, 2, j]
        for d in (2, 1, 3):
            step.append(send(mid.at[1, j, x_at[d]], got2.at[1, d - 1, j],
                             ss2.at[1, j, d - 1], sr2.at[1, j, d - 1], x_peer[d]))
        sums2.append(step)

    row = lax.broadcasted_iota(jnp.int32, (16, 128), 0) + chan * 16
    col = lax.broadcasted_iota(jnp.int32, (16, 128), 1)
    scale = jnp.sqrt(jnp.float32(32))
    for j in range(4):
        for copy in sums2[j]:
            copy.wait_recv()
        live = size_s[sector * 4 + targets[j]]
        for half, at in ((0, y), (1, x)):
            total = mid[half, j, at] + got2[half, 0, j] + got2[half, 1, j] + got2[half, 2, j]
            alive = jnp.logical_and(row < live, col + 128 * half < live)
            out[targets[j], :, 128 * half:128 * (half + 1)] = jnp.where(alive, total, 0.0) / scale

    for copy in sent:
        copy.wait_send()

    @pl.when(inner_sector)
    def _():
        for copy in sent_near:
            copy.wait_send()


def body(wave, left, right, source, shift, mask, size):
    f32, bf16, i32 = jnp.float32, jnp.bfloat16, jnp.int32
    dma = pltpu.SemaphoreType.DMA
    return pl.pallas_call(
        kernel,
        out_shape=jax.ShapeDtypeStruct((4, 16, 256), f32),
        in_specs=[pl.BlockSpec(memory_space=pl.ANY)] * 7,
        out_specs=pl.BlockSpec(memory_space=pltpu.VMEM),
        scratch_shapes=[
            pltpu.VMEM((2, 4, 4, 2, 16, 256), f32),
            pltpu.VMEM((2, 4, 4, 2, 16, 256), f32),
            pltpu.VMEM((4, 4, 2, 16, 256), f32),
            pltpu.VMEM((4, 4, 2, 16, 256), f32),
            pltpu.VMEM((2, 4, 256, 256), f32),
            pltpu.VMEM((2, 4, 256, 256), f32),
            pltpu.VMEM((2, 4, 256, 256), bf16),
            pltpu.VMEM((2, 4, 256, 256), bf16),
            pltpu.VMEM((2, 4, 256, 256), bf16),
            pltpu.VMEM((2, 4, 256, 256), bf16),
            pltpu.VMEM((4, 4, 4, 16, 128), f32),
            pltpu.VMEM((4, 4, 4, 16, 128), f32),
            pltpu.VMEM((2, 3, 4, 4, 16, 128), f32),
            pltpu.VMEM((2, 4, 4, 16, 128), f32),
            pltpu.VMEM((2, 3, 4, 16, 128), f32),
            pltpu.SMEM((5, 128), i32),
            pltpu.SMEM((32,), i32),
            pltpu.SMEM((32, 128), i32),
            pltpu.SMEM((128,), i32),
            dma((8,)),
            dma((2, 3)), dma((2, 3)), dma((2, 4, 3)), dma((2, 4, 3)),
            dma((2, 4)), dma((2, 4)), dma((2, 4, 2)), dma((2, 4, 2)),
            dma((2, 4)), dma((2, 4)), dma((2,)), dma((2,)),
            dma((2, 4, 3)), dma((2, 4, 3)), dma((2, 4, 3)), dma((2, 4, 3)),
        ],
        compiler_params=pltpu.CompilerParams(
            collective_id=0, has_side_effects=True, vmem_limit_bytes=53 * 2**20
        ),
        cost_estimate=pl.CostEstimate(
            flops=3 * 8 * 2 * 2 * 256**3, bytes_accessed=5 * 2**20, transcendentals=0
        ),
        name="heff",
    )(*[pltpu.with_memory_space_constraint(v, pltpu.HBM) for v in (wave, left, right, source, shift, mask, size)])


def solution(mesh):
    return jax.shard_map(
        body,
        mesh=mesh,
        in_specs=(
            P("sector", "chan", None),
            P("chan", "sector", None, None),
            P("chan", "sector", None, None),
            P(), P(), P(), P(),
        ),
        out_specs=P("sector", "chan", None),
        check_vma=False,
    )
```

```python
import functools

import jax
import jax.numpy as jnp
from jax import lax
from jax.experimental import pallas as pl
from jax.experimental.pallas import tpu as pltpu
from jax.sharding import PartitionSpec as P

MESH = pl.DeviceIdType.MESH
STEPS = (1, 3, 2)


def split(value):
    high = value.astype(jnp.bfloat16)
    low = (value - high.astype(jnp.float32)).astype(jnp.bfloat16)
    return high, low


def product(a_high, a_low, b_high, b_low):
    dot = functools.partial(jnp.dot, preferred_element_type=jnp.float32)
    return dot(a_high, b_high) + dot(a_high, b_low) + dot(a_low, b_high)


def kernel(
    wave, left, right, source, shift, mask, size, out,
    pair0, pair1, next0, next1, left_f, right_f, left_h, left_l, right_h, right_l,
    part0, part1, got, mid, got2, source_s, shift_s, mask_s, size_s,
    local_sem, s1, r1, s2, r2, zs, zr, n2s, n2r, twin_s, twin_r, near_s, near_r,
    ss1, sr1, ss2, sr2,
):
    sector = lax.axis_index("sector")
    chan = lax.axis_index("chan")
    z, core = sector // 2, lax.rem(sector, 2)
    x, y = chan // 4, lax.rem(chan, 4)

    x_at = [lax.rem(x + d, 4) for d in range(4)]
    y_at = [lax.rem(y + d, 4) for d in range(4)]
    x_peer = {d: (sector, x_at[d] * 4 + y) for d in STEPS}
    y_peer = {d: (sector, x * 4 + y_at[d]) for d in STEPS}
    twin = (z * 2 + 1 - core, chan)
    near = (lax.rem(sector + 2 * core - 1 + 32, 32), chan)
    targets = [3 - j + core * (2 * j - 3) for j in range(4)]
    kinds = (pair0.at[core], pair1.at[core])
    ends = (x_at, y_at)
    starts = (y_at, x_at)
    first_peer = (x_peer, y_peer)
    second_peer = (y_peer, x_peer)
    home = [wave.at[pl.ds(2 * core, 2)], wave.at[pl.ds(2 - 2 * core, 2)]]

    loads = [
        pltpu.make_async_copy(source, source_s, local_sem.at[0]),
        pltpu.make_async_copy(shift, shift_s, local_sem.at[1]),
        pltpu.make_async_copy(mask, mask_s, local_sem.at[2]),
        pltpu.make_async_copy(size, size_s, local_sem.at[3]),
    ]
    left_load = pltpu.make_async_copy(left, left_f, local_sem.at[4])
    right_load = pltpu.make_async_copy(right, right_f, local_sem.at[5])
    keeps = [
        pltpu.make_async_copy(home[0], pair0.at[core, y, x], local_sem.at[6]),
        pltpu.make_async_copy(home[1], pair1.at[core, x, y], local_sem.at[7]),
    ]
    for keep in keeps:
        keep.start()

    mine = [pair0.at[core, y, x], pair1.at[core, x, y]]
    barrier = pltpu.get_barrier_semaphore()
    partners = [x_peer[d] for d in STEPS] + [y_peer[d] for d in STEPS] + [twin]
    inner_sector = jnp.logical_and(sector > 0, sector < 31)

    @pl.when(inner_sector)
    def _():
        pl.semaphore_signal(barrier, inc=1, device_id=near, device_id_type=MESH)

    for partner in partners:
        pl.semaphore_signal(barrier, inc=1, device_id=partner, device_id_type=MESH)
    for keep in keeps:
        keep.wait()
    pl.semaphore_wait(barrier, len(partners) + inner_sector.astype(jnp.int32))

    sent, sent_near = [], []

    def planned(view, there, send_sem, recv_sem, device):
        return pltpu.make_async_remote_copy(
            src_ref=view, dst_ref=there, send_sem=send_sem, recv_sem=recv_sem,
            device_id=device, device_id_type=MESH,
        )

    def send(*where):
        copy = planned(*where)
        copy.start()
        sent.append(copy)
        return copy

    def send_near(copies):
        @pl.when(inner_sector)
        def _():
            for copy in copies:
                copy.start()

        sent_near.extend(copies)
        return copies

    def wait_near(copies):
        @pl.when(inner_sector)
        def _():
            for copy in copies:
                copy.wait_recv()

    first = {}
    for d in STEPS:
        for kind in range(2):
            first[kind, d] = send(
                mine[kind], kinds[kind].at[starts[kind][0], ends[kind][0]],
                s1.at[kind, d - 1], r1.at[kind, d - 1], first_peer[kind][d])

    nexts = (next0, next1)
    second, over, second_n = {}, {}, {}

    def piece(refs, kind, e):
        return refs[kind].at[starts[kind][0], ends[kind][(4 - e) % 4]]

    def pass_on(kind, e):
        here = piece(kinds, kind, e)
        for d in (2, 1, 3):
            second[kind, e, d] = send(
                here if e else mine[kind], here,
                s2.at[kind, e, d - 1], r2.at[kind, e, d - 1], second_peer[kind][d])

    def cross(kind, e):
        over[kind, e] = planned(piece(kinds, kind, e) if e else mine[kind], piece(nexts, kind, e),
                                zs.at[kind, e], zr.at[kind, e], near)
        send_near([over[kind, e]])

    def pass_on_n(e):
        for kind in range(2):
            here = piece(nexts, kind, e)
            for d in (1, 3):
                second_n[kind, e, d] = planned(
                    here, here, n2s.at[kind, e, d // 2], n2r.at[kind, e, d // 2],
                    second_peer[kind][d])
        copies = [second_n[kind, e, d] for kind in range(2) for d in (1, 3)]

        @pl.when(inner_sector)
        def _():
            for kind in range(2):
                over[kind, e].wait_recv()
                for d in (1, 3):
                    second_n[kind, e, d].start()

        sent_near.extend(copies)

    twins, groups = [], {}

    def group(kind, d):
        at = starts[kind][(4 - d) % 4]
        ref = kinds[kind].at[at]
        if d == 2:
            groups[kind] = planned(
                ref, nexts[kind].at[at], near_s.at[kind], near_r.at[kind], near)
            send_near([groups[kind]])
        twins.append(send(ref, ref, twin_s.at[kind, d], twin_r.at[kind, d], twin))

    for kind in range(2):
        cross(kind, 0)
    for kind in range(2):
        pass_on(kind, 0)
    left_load.start()
    right_load.start()
    for load in loads:
        load.start()
    left_load.wait()
    for w in range(2):
        for t in range(4):
            left_h[w, t], left_l[w, t] = split(left_f[w, t])
    right_load.wait()
    for w in range(2):
        for t in range(4):
            right_h[w, t], right_l[w, t] = split(right_f[w, t])
    for d in STEPS:
        for kind in range(2):
            first[kind, d].wait_recv()
            cross(kind, d)
            pass_on(kind, d)
        if d == 1:
            pass_on_n(0)
    pass_on_n(1)
    pass_on_n(3)
    for kind in range(2):
        group(kind, 0)
    pass_on_n(2)
    for d in (2, 1, 3):
        for kind in range(2):
            for e in range(4):
                second[kind, e, d].wait_recv()
            group(kind, d)
    for load in loads:
        load.wait()
    for copy in twins:
        copy.wait_recv()

    def assembled(ref, swapped):
        return jnp.concatenate(
            [ref(b, a) if swapped else ref(a, b) for a in range(4) for b in range(4)], axis=0)

    rows = lax.broadcasted_iota(jnp.int32, (256, 256), 0)
    cols = lax.broadcasted_iota(jnp.int32, (256, 256), 1)
    sums1 = []
    for j in range(4):
        if j % 2 == 0:
            kind = j // 2
            wait_near([groups[kind]] + [second_n[kind, e, d] for e in range(4) for d in (1, 3)])
        target = sector * 4 + targets[j]
        total = None
        for w in range(2):
            channel = chan * 2 + w
            s = source_s[shift_s[channel], target]
            live = size_s[s] * mask_s[channel, target]
            place = s - z * 8
            at = jnp.clip(place, 0, 7)
            owner, i, upper = at // 4, lax.rem(at, 2), lax.rem(at, 4) // 2
            block = jnp.where(
                upper == owner,
                assembled(lambda a, b: pair0[owner, a, b, i], True),
                assembled(lambda a, b: pair1[owner, a, b, i], False))
            for i in range(2):
                block = jnp.where(place == i - 2 + 10 * core,
                                  assembled(lambda a, b: next0[a, b, i], True), block)
            if j >= 2:
                for i in range(2):
                    block = jnp.where(place == i - 4 + 14 * core,
                                      assembled(lambda a, b: next1[a, b, i], False), block)
            block = jnp.where(jnp.logical_and(rows < live, cols < live), block, 0.0)
            inner = product(left_h[w, targets[j]], left_l[w, targets[j]], *split(block))
            term = product(*split(inner), right_h[w, targets[j]], right_l[w, targets[j]])
            total = term if total is None else total + term
        for a in range(4):
            for b in range(4):
                r = 64 * a + 16 * b
                part0[j, a, b] = total[r:r + 16, :128]
                part1[j, b, a] = total[r:r + 16, 128:]
        step = []
        for d in (2, 1, 3):
            step.append(send(part0.at[j, x_at[d]], got.at[0, d - 1, j],
                             ss1.at[0, j, d - 1], sr1.at[0, j, d - 1], x_peer[d]))
            step.append(send(part1.at[j, y_at[d]], got.at[1, d - 1, j],
                             ss1.at[1, j, d - 1], sr1.at[1, j, d - 1], y_peer[d]))
        sums1.append(step)

    sums2 = []
    for j in range(4):
        step = []
        for copy in sums1[j][0::2]:
            copy.wait_recv()
        mid[0, j] = part0[j, x] + got[0, 0, j] + got[0, 1, j] + got[0, 2, j]
        for d in (2, 1, 3):
            step.append(send(mid.at[0, j, y_at[d]], got2.at[0, d - 1, j],
                             ss2.at[0, j, d - 1], sr2.at[0, j, d - 1], y_peer[d]))
        for copy in sums1[j][1::2]:
            copy.wait_recv()
        mid[1, j] = part1[j, y] + got[1, 0, j] + got[1, 1, j] + got[1, 2, j]
        for d in (2, 1, 3):
            step.append(send(mid.at[1, j, x_at[d]], got2.at[1, d - 1, j],
                             ss2.at[1, j, d - 1], sr2.at[1, j, d - 1], x_peer[d]))
        sums2.append(step)

    row = lax.broadcasted_iota(jnp.int32, (16, 128), 0) + chan * 16
    col = lax.broadcasted_iota(jnp.int32, (16, 128), 1)
    scale = jnp.sqrt(jnp.float32(32))
    for j in range(4):
        for copy in sums2[j]:
            copy.wait_recv()
        live = size_s[sector * 4 + targets[j]]
        for half, at in ((0, y), (1, x)):
            total = mid[half, j, at] + got2[half, 0, j] + got2[half, 1, j] + got2[half, 2, j]
            alive = jnp.logical_and(row < live, col + 128 * half < live)
            out[targets[j], :, 128 * half:128 * (half + 1)] = jnp.where(alive, total, 0.0) / scale

    for copy in sent:
        copy.wait_send()

    @pl.when(inner_sector)
    def _():
        for copy in sent_near:
            copy.wait_send()


def body(wave, left, right, source, shift, mask, size):
    f32, bf16, i32 = jnp.float32, jnp.bfloat16, jnp.int32
    dma = pltpu.SemaphoreType.DMA
    return pl.pallas_call(
        kernel,
        out_shape=jax.ShapeDtypeStruct((4, 16, 256), f32),
        in_specs=[pl.BlockSpec(memory_space=pl.ANY)] * 7,
        out_specs=pl.BlockSpec(memory_space=pltpu.VMEM),
        scratch_shapes=[
            pltpu.VMEM((2, 4, 4, 2, 16, 256), f32),
            pltpu.VMEM((2, 4, 4, 2, 16, 256), f32),
            pltpu.VMEM((4, 4, 2, 16, 256), f32),
            pltpu.VMEM((4, 4, 2, 16, 256), f32),
            pltpu.VMEM((2, 4, 256, 256), f32),
            pltpu.VMEM((2, 4, 256, 256), f32),
            pltpu.VMEM((2, 4, 256, 256), bf16),
            pltpu.VMEM((2, 4, 256, 256), bf16),
            pltpu.VMEM((2, 4, 256, 256), bf16),
            pltpu.VMEM((2, 4, 256, 256), bf16),
            pltpu.VMEM((4, 4, 4, 16, 128), f32),
            pltpu.VMEM((4, 4, 4, 16, 128), f32),
            pltpu.VMEM((2, 3, 4, 4, 16, 128), f32),
            pltpu.VMEM((2, 4, 4, 16, 128), f32),
            pltpu.VMEM((2, 3, 4, 16, 128), f32),
            pltpu.SMEM((5, 128), i32),
            pltpu.SMEM((32,), i32),
            pltpu.SMEM((32, 128), i32),
            pltpu.SMEM((128,), i32),
            dma((8,)),
            dma((2, 3)), dma((2, 3)), dma((2, 4, 3)), dma((2, 4, 3)),
            dma((2, 4)), dma((2, 4)), dma((2, 4, 2)), dma((2, 4, 2)),
            dma((2, 4)), dma((2, 4)), dma((2,)), dma((2,)),
            dma((2, 4, 3)), dma((2, 4, 3)), dma((2, 4, 3)), dma((2, 4, 3)),
        ],
        compiler_params=pltpu.CompilerParams(
            collective_id=0, has_side_effects=True, vmem_limit_bytes=53 * 2**20
        ),
        cost_estimate=pl.CostEstimate(
            flops=3 * 8 * 2 * 2 * 256**3, bytes_accessed=5 * 2**20, transcendentals=0
        ),
        name="heff",
    )(*[pltpu.with_memory_space_constraint(v, pltpu.HBM) for v in (wave, left, right, source, shift, mask, size)])


def solution(mesh):
    return jax.shard_map(
        body,
        mesh=mesh,
        in_specs=(
            P("sector", "chan", None),
            P("chan", "sector", None, None),
            P("chan", "sector", None, None),
            P(), P(), P(), P(),
        ),
        out_specs=P("sector", "chan", None),
        check_vma=False,
    )
```

```python
import functools

import jax
import jax.numpy as jnp
from jax import lax
from jax.experimental import pallas as pl
from jax.experimental.pallas import tpu as pltpu
from jax.sharding import PartitionSpec as P

MESH = pl.DeviceIdType.MESH
STEPS = (1, 3, 2)


def split(value):
    high = value.astype(jnp.bfloat16)
    low = (value - high.astype(jnp.float32)).astype(jnp.bfloat16)
    return high, low


def product(a_high, a_low, b_high, b_low):
    dot = functools.partial(jnp.dot, preferred_element_type=jnp.float32)
    return dot(a_high, b_high) + dot(a_high, b_low) + dot(a_low, b_high)


def kernel(
    wave, left, right, source, shift, mask, size, out,
    pair0, pair1, next0, next1, left_f, right_f, left_h, left_l, right_h, right_l,
    part0, part1, got, mid, got2, source_s, shift_s, mask_s, size_s,
    local_sem, s1, r1, s2, r2, zs, zr, n2s, n2r, twin_s, twin_r, near_s, near_r,
    ss1, sr1, ss2, sr2,
):
    sector = lax.axis_index("sector")
    chan = lax.axis_index("chan")
    z, core = sector // 2, lax.rem(sector, 2)
    x, y = chan // 4, lax.rem(chan, 4)

    x_at = [lax.rem(x + d, 4) for d in range(4)]
    y_at = [lax.rem(y + d, 4) for d in range(4)]
    x_peer = {d: (sector, x_at[d] * 4 + y) for d in STEPS}
    y_peer = {d: (sector, x * 4 + y_at[d]) for d in STEPS}
    twin = (z * 2 + 1 - core, chan)
    near = (lax.rem(sector + 2 * core - 1 + 32, 32), chan)
    targets = [3 - j + core * (2 * j - 3) for j in range(4)]
    kinds = (pair0.at[core], pair1.at[core])
    ends = (x_at, y_at)
    starts = (y_at, x_at)
    first_peer = (x_peer, y_peer)
    second_peer = (y_peer, x_peer)
    home = [wave.at[pl.ds(2 * core, 2)], wave.at[pl.ds(2 - 2 * core, 2)]]

    loads = [
        pltpu.make_async_copy(source, source_s, local_sem.at[0]),
        pltpu.make_async_copy(shift, shift_s, local_sem.at[1]),
        pltpu.make_async_copy(mask, mask_s, local_sem.at[2]),
        pltpu.make_async_copy(size, size_s, local_sem.at[3]),
    ]
    left_load = pltpu.make_async_copy(left, left_f, local_sem.at[4])
    right_load = pltpu.make_async_copy(right, right_f, local_sem.at[5])
    keeps = [
        pltpu.make_async_copy(home[0], pair0.at[core, y, x], local_sem.at[6]),
        pltpu.make_async_copy(home[1], pair1.at[core, x, y], local_sem.at[7]),
    ]
    for keep in keeps:
        keep.start()

    mine = [pair0.at[core, y, x], pair1.at[core, x, y]]
    barrier = pltpu.get_barrier_semaphore()
    partners = [x_peer[d] for d in STEPS] + [y_peer[d] for d in STEPS] + [twin]
    inner_sector = jnp.logical_and(sector > 0, sector < 31)

    @pl.when(inner_sector)
    def _():
        pl.semaphore_signal(barrier, inc=1, device_id=near, device_id_type=MESH)

    for partner in partners:
        pl.semaphore_signal(barrier, inc=1, device_id=partner, device_id_type=MESH)
    for keep in keeps:
        keep.wait()
    pl.semaphore_wait(barrier, len(partners) + inner_sector.astype(jnp.int32))

    sent, sent_near = [], []

    def planned(view, there, send_sem, recv_sem, device):
        return pltpu.make_async_remote_copy(
            src_ref=view, dst_ref=there, send_sem=send_sem, recv_sem=recv_sem,
            device_id=device, device_id_type=MESH,
        )

    def send(*where):
        copy = planned(*where)
        copy.start()
        sent.append(copy)
        return copy

    def send_near(copies):
        @pl.when(inner_sector)
        def _():
            for copy in copies:
                copy.start()

        sent_near.extend(copies)
        return copies

    def wait_near(copies):
        @pl.when(inner_sector)
        def _():
            for copy in copies:
                copy.wait_recv()

    first = {}
    for d in STEPS:
        for kind in range(2):
            first[kind, d] = send(
                mine[kind], kinds[kind].at[starts[kind][0], ends[kind][0]],
                s1.at[kind, d - 1], r1.at[kind, d - 1], first_peer[kind][d])

    nexts = (next0, next1)
    second, over, second_n = {}, {}, {}

    def piece(refs, kind, e):
        return refs[kind].at[starts[kind][0], ends[kind][(4 - e) % 4]]

    def pass_on(kind, e):
        here = piece(kinds, kind, e)
        for d in (2, 1, 3):
            second[kind, e, d] = send(
                here if e else mine[kind], here,
                s2.at[kind, e, d - 1], r2.at[kind, e, d - 1], second_peer[kind][d])

    def cross(kind, e):
        over[kind, e] = planned(piece(kinds, kind, e) if e else mine[kind], piece(nexts, kind, e),
                                zs.at[kind, e], zr.at[kind, e], near)
        send_near([over[kind, e]])

    def pass_on_n(e):
        for kind in range(2):
            here = piece(nexts, kind, e)
            for d in (1, 3):
                second_n[kind, e, d] = planned(
                    here, here, n2s.at[kind, e, d // 2], n2r.at[kind, e, d // 2],
                    second_peer[kind][d])
        copies = [second_n[kind, e, d] for kind in range(2) for d in (1, 3)]

        @pl.when(inner_sector)
        def _():
            for kind in range(2):
                over[kind, e].wait_recv()
                for d in (1, 3):
                    second_n[kind, e, d].start()

        sent_near.extend(copies)

    twins, groups = [], {}

    def group(kind, d):
        at = starts[kind][(4 - d) % 4]
        ref = kinds[kind].at[at]
        if d == 2:
            groups[kind] = planned(
                ref, nexts[kind].at[at], near_s.at[kind], near_r.at[kind], near)
            send_near([groups[kind]])
        twins.append(send(ref, ref, twin_s.at[kind, d], twin_r.at[kind, d], twin))

    for kind in range(2):
        cross(kind, 0)
    for kind in range(2):
        pass_on(kind, 0)
    left_load.start()
    right_load.start()
    for load in loads:
        load.start()
    for d in STEPS:
        for kind in range(2):
            first[kind, d].wait_recv()
            cross(kind, d)
            pass_on(kind, d)
    for kind in range(2):
        group(kind, 0)
    left_load.wait()
    for w in range(2):
        for t in range(4):
            left_h[w, t], left_l[w, t] = split(left_f[w, t])
    for e in (0,) + STEPS:
        pass_on_n(e)
    right_load.wait()
    for w in range(2):
        for t in range(4):
            right_h[w, t], right_l[w, t] = split(right_f[w, t])
    for d in (2, 1, 3):
        for kind in range(2):
            for e in range(4):
                second[kind, e, d].wait_recv()
            group(kind, d)
    for load in loads:
        load.wait()
    for copy in twins:
        copy.wait_recv()

    def assembled(ref, swapped):
        return jnp.concatenate(
            [ref(b, a) if swapped else ref(a, b) for a in range(4) for b in range(4)], axis=0)

    rows = lax.broadcasted_iota(jnp.int32, (256, 256), 0)
    cols = lax.broadcasted_iota(jnp.int32, (256, 256), 1)
    sums1 = []
    for j in range(4):
        if j % 2 == 0:
            kind = j // 2
            wait_near([groups[kind]] + [second_n[kind, e, d] for e in range(4) for d in (1, 3)])
        target = sector * 4 + targets[j]
        total = None
        for w in range(2):
            channel = chan * 2 + w
            s = source_s[shift_s[channel], target]
            live = size_s[s] * mask_s[channel, target]
            place = s - z * 8
            at = jnp.clip(place, 0, 7)
            owner, i, upper = at // 4, lax.rem(at, 2), lax.rem(at, 4) // 2
            block = jnp.where(
                upper == owner,
                assembled(lambda a, b: pair0[owner, a, b, i], True),
                assembled(lambda a, b: pair1[owner, a, b, i], False))
            for i in range(2):
                block = jnp.where(place == i - 2 + 10 * core,
                                  assembled(lambda a, b: next0[a, b, i], True), block)
            if j >= 2:
                for i in range(2):
                    block = jnp.where(place == i - 4 + 14 * core,
                                      assembled(lambda a, b: next1[a, b, i], False), block)
            block = jnp.where(jnp.logical_and(rows < live, cols < live), block, 0.0)
            inner = product(left_h[w, targets[j]], left_l[w, targets[j]], *split(block))
            term = product(*split(inner), right_h[w, targets[j]], right_l[w, targets[j]])
            total = term if total is None else total + term
        for a in range(4):
            for b in range(4):
                r = 64 * a + 16 * b
                part0[j, a, b] = total[r:r + 16, :128]
                part1[j, b, a] = total[r:r + 16, 128:]
        step = []
        for d in (2, 1, 3):
            step.append(send(part0.at[j, x_at[d]], got.at[0, d - 1, j],
                             ss1.at[0, j, d - 1], sr1.at[0, j, d - 1], x_peer[d]))
            step.append(send(part1.at[j, y_at[d]], got.at[1, d - 1, j],
                             ss1.at[1, j, d - 1], sr1.at[1, j, d - 1], y_peer[d]))
        sums1.append(step)

    sums2 = []
    for j in range(4):
        step = []
        for copy in sums1[j][0::2]:
            copy.wait_recv()
        mid[0, j] = part0[j, x] + got[0, 0, j] + got[0, 1, j] + got[0, 2, j]
        for d in (2, 1, 3):
            step.append(send(mid.at[0, j, y_at[d]], got2.at[0, d - 1, j],
                             ss2.at[0, j, d - 1], sr2.at[0, j, d - 1], y_peer[d]))
        for copy in sums1[j][1::2]:
            copy.wait_recv()
        mid[1, j] = part1[j, y] + got[1, 0, j] + got[1, 1, j] + got[1, 2, j]
        for d in (2, 1, 3):
            step.append(send(mid.at[1, j, x_at[d]], got2.at[1, d - 1, j],
                             ss2.at[1, j, d - 1], sr2.at[1, j, d - 1], x_peer[d]))
        sums2.append(step)

    row = lax.broadcasted_iota(jnp.int32, (16, 128), 0) + chan * 16
    col = lax.broadcasted_iota(jnp.int32, (16, 128), 1)
    scale = jnp.sqrt(jnp.float32(32))
    for j in range(4):
        for copy in sums2[j]:
            copy.wait_recv()
        live = size_s[sector * 4 + targets[j]]
        for half, at in ((0, y), (1, x)):
            total = mid[half, j, at] + got2[half, 0, j] + got2[half, 1, j] + got2[half, 2, j]
            alive = jnp.logical_and(row < live, col + 128 * half < live)
            out[targets[j], :, 128 * half:128 * (half + 1)] = jnp.where(alive, total, 0.0) / scale

    for copy in sent:
        copy.wait_send()

    @pl.when(inner_sector)
    def _():
        for copy in sent_near:
            copy.wait_send()


def body(wave, left, right, source, shift, mask, size):
    f32, bf16, i32 = jnp.float32, jnp.bfloat16, jnp.int32
    dma = pltpu.SemaphoreType.DMA
    return pl.pallas_call(
        kernel,
        out_shape=jax.ShapeDtypeStruct((4, 16, 256), f32),
        in_specs=[pl.BlockSpec(memory_space=pl.ANY)] * 7,
        out_specs=pl.BlockSpec(memory_space=pltpu.VMEM),
        scratch_shapes=[
            pltpu.VMEM((2, 4, 4, 2, 16, 256), f32),
            pltpu.VMEM((2, 4, 4, 2, 16, 256), f32),
            pltpu.VMEM((4, 4, 2, 16, 256), f32),
            pltpu.VMEM((4, 4, 2, 16, 256), f32),
            pltpu.VMEM((2, 4, 256, 256), f32),
            pltpu.VMEM((2, 4, 256, 256), f32),
            pltpu.VMEM((2, 4, 256, 256), bf16),
            pltpu.VMEM((2, 4, 256, 256), bf16),
            pltpu.VMEM((2, 4, 256, 256), bf16),
            pltpu.VMEM((2, 4, 256, 256), bf16),
            pltpu.VMEM((4, 4, 4, 16, 128), f32),
            pltpu.VMEM((4, 4, 4, 16, 128), f32),
            pltpu.VMEM((2, 3, 4, 4, 16, 128), f32),
            pltpu.VMEM((2, 4, 4, 16, 128), f32),
            pltpu.VMEM((2, 3, 4, 16, 128), f32),
            pltpu.SMEM((5, 128), i32),
            pltpu.SMEM((32,), i32),
            pltpu.SMEM((32, 128), i32),
            pltpu.SMEM((128,), i32),
            dma((8,)),
            dma((2, 3)), dma((2, 3)), dma((2, 4, 3)), dma((2, 4, 3)),
            dma((2, 4)), dma((2, 4)), dma((2, 4, 2)), dma((2, 4, 2)),
            dma((2, 4)), dma((2, 4)), dma((2,)), dma((2,)),
            dma((2, 4, 3)), dma((2, 4, 3)), dma((2, 4, 3)), dma((2, 4, 3)),
        ],
        compiler_params=pltpu.CompilerParams(
            collective_id=0, has_side_effects=True, vmem_limit_bytes=53 * 2**20
        ),
        cost_estimate=pl.CostEstimate(
            flops=3 * 8 * 2 * 2 * 256**3, bytes_accessed=5 * 2**20, transcendentals=0
        ),
        name="heff",
    )(*[pltpu.with_memory_space_constraint(v, pltpu.HBM) for v in (wave, left, right, source, shift, mask, size)])


def solution(mesh):
    return jax.shard_map(
        body,
        mesh=mesh,
        in_specs=(
            P("sector", "chan", None),
            P("chan", "sector", None, None),
            P("chan", "sector", None, None),
            P(), P(), P(), P(),
        ),
        out_specs=P("sector", "chan", None),
        check_vma=False,
    )
```
